32 devices in a mesh: filt: 16 (over z, y, x), slab: 2 (over core).
Axes of the slice: x: 2, y: 2, z: 4, core: 2. Of those that a mesh axis runs over, the one named last changes fastest.
Arguments:
- activations: bfloat16 [512, 4, 512], P('filt', 'slab'), may hold values from -6 to 6
- grad_out: bfloat16 [512, 4, 512], P('filt', 'slab'), may hold values from -6 to 6
- weights: bfloat16 [27, 256, 256], P(None, 'filt'), may hold values from -0.078125 to 0.078125
Outputs:
- out_map: bfloat16 [512, 4, 512], P('filt', 'slab')
- grad_in: bfloat16 [512, 4, 512], P('filt', 'slab')
- filter_grad: float32 [27, 256, 256], P(None, 'filt')
The draws below stay inside these ranges and needn't reach their ends.
All inputs are finite; a program needn't handle non-finite values.
Results may differ from the reference program's by a relative error of at most 0.001.
Values may be sent and summed in bfloat16 or wider, within the bound.
A program may use at most 64 MiB of HBM per device.

```python
import math
import jax
import jax.numpy as jnp
from jax import lax

CH_IN = 256
CH_OUT = 256
GROUPS = 8
ROWS = 8
WIDTH = 64
ROW_BLOCKS = 2
HEIGHT = 16
DEPTH_ALL = 4
N_FILT = 16


def block_scale(own_key, dims, shards, low, top_value):
    def one(position, blocks):
        steps = jax.random.uniform(jax.random.fold_in(jax.random.fold_in(own_key, 6), position), (blocks,), jnp.float32, low / len(shards), top_value / len(shards))
        return jnp.repeat(jnp.exp(steps), dims[position] // blocks).reshape((-1,) + (1,) * (len(dims) - position - 1))

    loudness = one(*shards[0])
    for cut in shards[1:]:
        loudness = loudness * one(*cut)
    return loudness


def centred(rng, shape, spread, reach, shards=(), kind=jnp.bfloat16):
    drawn = jax.random.normal(rng, shape, jnp.float32) * spread
    if len(shards) > 0:
        drawn = block_scale(rng, shape, shards, -0.22, 0.18) * drawn
    return jnp.clip(drawn, min=-reach, max=reach).astype(kind)


def setup_inputs(seed: int = 0) -> dict:
    key_of = jax.random.split(jax.random.key(seed), 4)
    return {
        "activations": centred(key_of[0], (ROW_BLOCKS * CH_IN, DEPTH_ALL, ROWS * WIDTH), 1.0, 6.0, ((0, 16), (1, 2))),
        "grad_out": centred(key_of[1], (ROW_BLOCKS * CH_OUT, DEPTH_ALL, ROWS * WIDTH), 1.0, 6.0, ((0, 16), (1, 2))),
        "weights": centred(key_of[2], (27, CH_OUT, CH_IN), (27 * CH_IN) ** -0.5, 0.078125, ((1, 16),)),
    }


def to_volume(array, chans):
    shaped = array.reshape(ROW_BLOCKS, GROUPS, chans // GROUPS, DEPTH_ALL, ROWS, WIDTH)
    return jnp.transpose(shaped, (1, 2, 3, 0, 4, 5)).reshape(chans, DEPTH_ALL, HEIGHT, WIDTH)

def from_volume(volume, chans):
    shaped = volume.reshape(GROUPS, chans // GROUPS, DEPTH_ALL, ROW_BLOCKS, ROWS, WIDTH)
    return jnp.transpose(shaped, (3, 0, 1, 2, 4, 5)).reshape(ROW_BLOCKS * chans, DEPTH_ALL, ROWS * WIDTH)

def rows_natural(array):
    shaped = array.reshape(27, ROW_BLOCKS, GROUPS, CH_OUT // N_FILT, CH_IN)
    return jnp.transpose(shaped, (0, 2, 1, 3, 4)).reshape(27, CH_OUT, CH_IN)

def rows_stored(array):
    shaped = array.reshape(27, GROUPS, ROW_BLOCKS, CH_OUT // N_FILT, CH_IN)
    return jnp.transpose(shaped, (0, 2, 1, 3, 4)).reshape(27, CH_OUT, CH_IN)

def shifted(padded, plane_off, row_off, col_off):
    window = padded[:, plane_off:plane_off + DEPTH_ALL, row_off:row_off + HEIGHT, col_off:col_off + WIDTH]
    return window.reshape(window.shape[0], -1)

def reference(activations, grad_out, weights):
    weights = rows_natural(weights)
    volume_in = to_volume(activations, CH_IN)
    volume_grad = to_volume(grad_out, CH_OUT)
    padded_in = jnp.pad(volume_in, ((0, 0), (1, 1), (1, 1), (1, 1)))
    padded_grad = jnp.pad(volume_grad, ((0, 0), (1, 1), (1, 1), (1, 1)))
    flat_grad = volume_grad.reshape(CH_OUT, -1)
    output_sum = jnp.zeros((CH_OUT, DEPTH_ALL * HEIGHT * WIDTH), jnp.float32)
    input_sum = jnp.zeros((CH_IN, DEPTH_ALL * HEIGHT * WIDTH), jnp.float32)
    filter_list = []
    for plane_off in range(3):
        for row_off in range(3):
            for col_off in range(3):
                tap = 9 * plane_off + 3 * row_off + col_off
                tap_input = shifted(padded_in, plane_off, row_off, col_off)
                output_sum = output_sum + jnp.dot(weights[tap], tap_input, preferred_element_type=jnp.float32)
                filter_list.append(lax.dot_general(flat_grad, tap_input, (((1,), (1,)), ((), ())), preferred_element_type=jnp.float32))
                tap_grad = shifted(padded_grad, 2 - plane_off, 2 - row_off, 2 - col_off)
                input_sum = input_sum + lax.dot_general(weights[tap], tap_grad, (((0,), (0,)), ((), ())), preferred_element_type=jnp.float32)
    scale_factor = 1.0 / math.sqrt(DEPTH_ALL * HEIGHT * WIDTH)
    filter_grad = rows_stored(jnp.stack(filter_list, axis=0) * scale_factor)
    out_map = from_volume(output_sum.astype(jnp.bfloat16).reshape(CH_OUT, DEPTH_ALL, HEIGHT, WIDTH), CH_OUT)
    grad_in = from_volume(input_sum.astype(jnp.bfloat16).reshape(CH_IN, DEPTH_ALL, HEIGHT, WIDTH), CH_IN)
    return (out_map, grad_in, filter_grad)
```

```python
import math

import jax
import jax.numpy as jnp
from jax import lax
from jax.experimental import pallas as pl
from jax.experimental.pallas import tpu as pltpu
from jax.sharding import PartitionSpec as P

CH_IN = 256
CH_OUT = 256
GROUPS = 8
ROWS = 8
WIDTH = 64


def extended(shard, sides, width):
    for axis, dim in sides:
        count, length = (lax.axis_size(axis), shard.shape[dim])
        up = [(i, (i + 1) % count) for i in range(count - 1)]
        down = [(j, i) for i, j in up]
        last = lax.slice_in_dim(shard, length - width, length, axis=dim)
        initial = lax.slice_in_dim(shard, 0, width, axis=dim)
        before = lax.ppermute(last, axis, up)
        after = lax.ppermute(initial, axis, down)
        shard = jnp.concatenate([before, shard, after], axis=dim)
    return shard


def shifted(block, axis, distance):
    devices = range(lax.axis_size(axis))
    route = [(i - distance, i) for i in devices if i - distance in devices]
    return lax.ppermute(block, axis, route)


def from_partner(value, axis, apart):
    mask = 2**apart
    pairs = [(source, source ^ mask) for source in range(lax.axis_size(axis))]
    return lax.ppermute(value, axis, pairs)


def correlate(image, kernel, lhs_spec):
    return lax.conv_general_dilated(
        image,
        kernel,
        (1, 1, 1),
        ((0, 0), (0, 0), (1, 1)),
        dimension_numbers=(lhs_spec, "OIDHW", "NCDHW"),
        preferred_element_type=jnp.float32,
    )


def pad_block(pieces):
    chan_count = pieces.shape[0]
    depth_dev = pieces.shape[1]
    deepened = extended(pieces, (("slab", 1),), 1)
    planes_grid = deepened.reshape(chan_count, depth_dev + 2, ROWS, WIDTH)
    blocks_all = lax.axis_size("filt") // GROUPS
    row_pos = lax.axis_index("filt") // GROUPS
    from_below = shifted(planes_grid[:, :, ROWS - 1 :], "filt", GROUPS)
    from_above = shifted(planes_grid[:, :, :1], "filt", -GROUPS)
    from_below = jnp.where(row_pos == 0, jnp.zeros_like(from_below), from_below)
    from_above = jnp.where(row_pos == blocks_all - 1, jnp.zeros_like(from_above), from_above)
    return jnp.concatenate([from_below, planes_grid, from_above], axis=2)


def gather_groups(pieces):
    my_index = lax.axis_index("filt")
    for bit_num in range(GROUPS.bit_length() - 1):
        partner = from_partner(pieces, "filt", bit_num)
        upper_side = my_index // (1 << bit_num) % 2 == 1
        lower_part = jnp.where(upper_side, partner, pieces)
        upper_part = jnp.where(upper_side, pieces, partner)
        pieces = jnp.concatenate([lower_part, upper_part], axis=0)
    return pieces


def gather_blocks(pieces, axis_dim):
    blocks_all = lax.axis_size("filt") // GROUPS
    group_bits = GROUPS.bit_length() - 1
    my_index = lax.axis_index("filt")
    for section_num in range(blocks_all.bit_length() - 1):
        bit_num = group_bits + section_num
        partner = from_partner(pieces, "filt", bit_num)
        upper_side = my_index // (1 << bit_num) % 2 == 1
        lower_part = jnp.where(upper_side, partner, pieces)
        upper_part = jnp.where(upper_side, pieces, partner)
        pieces = jnp.concatenate([lower_part, upper_part], axis=axis_dim)
    return pieces


def reduce_halves(partial_value):
    blocks_all = lax.axis_size("filt") // GROUPS
    bits_count = blocks_all.bit_length() - 1
    group_bits = GROUPS.bit_length() - 1
    my_index = lax.axis_index("filt")
    for section_num in range(bits_count):
        bit_num = group_bits + bits_count - 1 - section_num
        half_size = partial_value.shape[1] // 2
        lower_part = partial_value[:, :half_size]
        upper_part = partial_value[:, half_size:]
        upper_side = my_index // (1 << bit_num) % 2 == 1
        sending = jnp.where(upper_side, lower_part, upper_part)
        keeping = jnp.where(upper_side, upper_part, lower_part)
        partial_value = keeping + from_partner(sending, "filt", bit_num)
    return partial_value


def per_device_general(activations, grad_out, weights):
    chan_local = activations.shape[0]
    depth_dev = activations.shape[1]
    blocks_all = lax.axis_size("filt") // GROUPS
    rows_dev = weights.shape[1]
    depth_all = depth_dev * lax.axis_size("slab")
    height_all = ROWS * blocks_all
    whole_in = gather_groups(pad_block(activations))
    whole_grad = gather_groups(pad_block(grad_out))
    group_weights = gather_blocks(weights, 1)
    reordered = jnp.transpose(
        weights.reshape(27, rows_dev, GROUPS, blocks_all, rows_dev), (0, 1, 3, 2, 4)
    ).reshape(27, rows_dev, CH_IN)
    stored_rows = gather_blocks(
        lax.all_to_all(reordered, "filt", split_axis=2, concat_axis=1, tiled=True), 2
    )
    column_weights = jnp.transpose(
        stored_rows.reshape(27, blocks_all, GROUPS, rows_dev, chan_local), (0, 2, 1, 3, 4)
    ).reshape(27, CH_OUT, chan_local)
    out_kernel = jnp.transpose(group_weights, (1, 2, 0)).reshape(chan_local, CH_IN, 3, 3, 3)
    output_sum = correlate(whole_in[None], out_kernel, "NCDHW")
    grad_kernel = grad_out.reshape(chan_local, 1, depth_dev, ROWS, WIDTH)
    filter_terms = correlate(whole_in[:, None], grad_kernel, "NCDHW")
    filter_part = jnp.transpose(filter_terms.reshape(CH_IN, chan_local, 27), (2, 1, 0))
    in_kernel = jnp.transpose(column_weights[::-1], (2, 1, 0)).reshape(chan_local, CH_OUT, 3, 3, 3)
    input_sum = correlate(whole_grad[None], in_kernel, "NCDHW")
    scale_factor = 1.0 / math.sqrt(depth_all * height_all * WIDTH)
    filter_grad = lax.psum(reduce_halves(filter_part), "slab") * scale_factor
    out_map = output_sum.astype(jnp.bfloat16).reshape(chan_local, depth_dev, ROWS * WIDTH)
    grad_in = input_sum.astype(jnp.bfloat16).reshape(chan_local, depth_dev, ROWS * WIDTH)
    return (out_map, grad_in, filter_grad)


PLANE = ROWS * WIDTH
LOCAL = CH_IN // GROUPS
HALO = 128
MESH = pl.DeviceIdType.MESH


def spread(total, low_from):
    column = lax.broadcasted_iota(jnp.int32, (LOCAL, PLANE), 1) % WIDTH
    first, middle, last = (total[k * LOCAL : (k + 1) * LOCAL] for k in range(3))
    if not low_from:
        first, last = last, first
    up = jnp.where(column == 0, 0.0, pltpu.roll(first, 1, 1))
    down = jnp.where(column == WIDTH - 1, 0.0, pltpu.roll(last, PLANE - 1, 1))
    return up + middle + down


def fused_kernel(
    scale, act, grad, own_w, own_wt, out, gin, fgrad,
    vol_in, vol_grad, halo, halo_own, group_w, column_w, shifts,
    terms, terms_core, cross_out, cross_in, half_own, half_in,
    send, recv,
):
    me = lax.axis_index("filt")
    slab = lax.axis_index("slab")
    block, group = me // GROUPS, me % GROUPS
    other_slab = 1 - slab
    across = (1 - block) * GROUPS + group
    rows = own_w.shape[1]

    def remote(src, dst, sem, filt, core):
        return pltpu.make_async_remote_copy(
            src_ref=src, dst_ref=dst, send_sem=send.at[sem], recv_sem=recv.at[sem],
            device_id=(filt, core), device_id_type=MESH,
        )

    def aligned(index, size):
        return pl.ds(pl.multiple_of(index * size, size), size)

    peers = [block * GROUPS + (group + k) % GROUPS for k in range(1, GROUPS)]
    others = [(me + k) % (2 * GROUPS) for k in range(1, 2 * GROUPS)]
    barrier = pltpu.get_barrier_semaphore()
    for device in others:
        pl.semaphore_signal(barrier, inc=1, device_id=(device, slab), device_id_type=MESH)
    pl.semaphore_signal(barrier, inc=1, device_id=(me, other_slab), device_id_type=MESH)

    channels = aligned(group, LOCAL)
    edge = pl.ds(pl.multiple_of((1 - block) * (PLANE - HALO), HALO), HALO)
    halo_own[0] = act[:, :, edge]
    halo_own[1] = grad[:, :, edge]
    pl.semaphore_wait(barrier, 2 * GROUPS)

    halo_copy = remote(halo_own, halo.at[:, 1:3, channels, :], 0, across, slab)
    halo_copy.start()
    act_copies = [
        remote(act, vol_in.at[1:3, 1, channels, :], 8 + k, peer, slab)
        for k, peer in enumerate(peers)
    ]
    for copy in act_copies:
        copy.start()
    group_copy = remote(own_w, group_w.at[:, aligned(block, rows), :], 22, across, slab)
    group_copy.start()
    grad_copies = [
        remote(grad, vol_grad.at[1:3, 1, channels, :], 15 + k, peer, slab)
        for k, peer in enumerate(peers)
    ]
    for copy in grad_copies:
        copy.start()
    mine = aligned(group * 2 + block, rows)
    column_copies = [
        remote(own_wt.at[device % GROUPS], column_w.at[:, mine, :], 23 + k, device, slab)
        for k, device in enumerate(others)
    ]
    for copy in column_copies:
        copy.start()

    zero_plane = 3 * slab
    vol_in[zero_plane, 1] = jnp.zeros((CH_IN, PLANE), jnp.bfloat16)
    vol_grad[zero_plane, 1] = jnp.zeros((CH_IN, PLANE), jnp.bfloat16)
    halo[:, zero_plane] = jnp.zeros((2, CH_IN, HALO), jnp.bfloat16)
    vol_in[1:3, 1, channels, :] = act[...]
    vol_grad[1:3, 1, channels, :] = grad[...]
    group_w[:, aligned(block, rows), :] = own_w[...]
    column_w[:, mine, :] = own_wt[group]
    column = lax.broadcasted_iota(jnp.int32, (LOCAL, PLANE), 1) % WIDTH
    for depth in range(2):
        value = grad[depth].astype(jnp.float32)
        lower = jnp.where(column == WIDTH - 1, 0.0, pltpu.roll(value, PLANE - 1, 1))
        upper = jnp.where(column == 0, 0.0, pltpu.roll(value, 1, 1))
        shifts[depth, 0:LOCAL] = lower.astype(jnp.bfloat16)
        shifts[depth, LOCAL : 2 * LOCAL] = grad[depth]
        shifts[depth, 2 * LOCAL :] = upper.astype(jnp.bfloat16)

    halo_copy.wait_recv()
    halo_copies = [
        remote(halo.at[:, 1:3, channels, :], halo.at[:, 1:3, channels, :], 1 + k, peer, slab)
        for k, peer in enumerate(peers)
    ]
    for copy in halo_copies:
        copy.start()

    gives, takes = 2 - slab, 3 * slab
    for copy in act_copies:
        copy.wait_recv()
    act_plane = remote(vol_in.at[gives, 1], vol_in.at[takes, 1], 38, me, other_slab)
    act_plane.start()
    for copy in halo_copies:
        copy.wait_recv()
    halo_plane = remote(halo.at[:, gives], halo.at[:, takes], 39, me, other_slab)
    halo_plane.start()

    def shift_rows(volume, which, plane):
        edges = halo[which, plane]
        none = jnp.zeros_like(edges)
        whole = jnp.concatenate(
            [jnp.where(block == 1, edges, none), volume[plane, 1], jnp.where(block == 0, edges, none)],
            axis=1,
        )
        volume[plane, 0] = whole[:, HALO - WIDTH : HALO - WIDTH + PLANE]
        volume[plane, 2] = whole[:, HALO + WIDTH : HALO + WIDTH + PLANE]

    shift_rows(vol_in, 0, 1)
    shift_rows(vol_in, 0, 2)
    act_plane.wait_recv()
    halo_plane.wait_recv()
    shift_rows(vol_in, 0, 0)
    shift_rows(vol_in, 0, 3)

    over_cells = (((1,), (1,)), ((), ()))
    half = CH_IN // 2
    for pair in range(9):
        a, b = pair // 3, pair % 3
        total = sum(
            lax.dot_general(
                shifts[depth], vol_in[depth + a, b], over_cells, preferred_element_type=jnp.float32
            )
            for depth in range(2)
        )
        for c in range(3):
            for dest in range(2):
                low = c * LOCAL + dest * rows
                for side in range(2):
                    terms[side, dest, 3 * pair + c] = total[
                        low : low + rows, side * half : (side + 1) * half
                    ]
    terms_copy = remote(terms.at[other_slab], terms_core, 41, me, other_slab)
    terms_copy.start()

    group_copy.wait_recv()
    for depth in range(2):
        total = jnp.zeros((3 * LOCAL, PLANE), jnp.float32)
        for pair in range(9):
            filters = group_w[3 * pair : 3 * pair + 3].reshape(3 * LOCAL, CH_IN)
            total += jnp.dot(
                filters, vol_in[depth + pair // 3, pair % 3], preferred_element_type=jnp.float32
            )
        out[depth] = spread(total, True).astype(out.dtype)

    terms_copy.wait_recv()
    cross_out[...] = terms[slab, 1 - block] + terms_core[1 - block]
    cross = remote(cross_out, cross_in, 42, across, slab)
    cross.start()

    for copy in grad_copies:
        copy.wait_recv()
    grad_plane = remote(vol_grad.at[gives, 1], vol_grad.at[takes, 1], 40, me, other_slab)
    grad_plane.start()
    shift_rows(vol_grad, 1, 1)
    shift_rows(vol_grad, 1, 2)
    grad_plane.wait_recv()
    shift_rows(vol_grad, 1, 0)
    shift_rows(vol_grad, 1, 3)
    for copy in column_copies:
        copy.wait_recv()
    over_rows = (((0,), (0,)), ((), ()))
    totals = [jnp.zeros((HALO, PLANE), jnp.float32) for _ in range(2)]
    for pair in range(9):
        filters = column_w[pair]
        for depth in range(2):
            totals[depth] += lax.dot_general(
                filters, vol_grad[depth + 2 - pair // 3, 2 - pair % 3], over_rows,
                preferred_element_type=jnp.float32,
            )
    for depth in range(2):
        gin[depth] = spread(totals[depth], False).astype(gin.dtype)

    cross.wait_recv()
    half_own[...] = (terms[slab, block] + terms_core[block] + cross_in[...]) * scale
    share = remote(half_own, half_in, 43, me, other_slab)
    share.start()
    fgrad[:, :, aligned(slab, half)] = half_own[...]
    share.wait_recv()
    fgrad[:, :, aligned(other_slab, half)] = half_in[...]

    for copy in (
        [halo_copy, group_copy, act_plane, halo_plane, grad_plane, terms_copy, cross, share]
        + halo_copies + act_copies + grad_copies + column_copies
    ):
        copy.wait_send()


def per_device_paired(activations, grad_out, weights):
    depth_dev = activations.shape[1]
    rows = weights.shape[1]
    cells = depth_dev * 2 * ROWS * 2 * WIDTH
    packed = jnp.transpose(
        weights.reshape(9, 3, rows, GROUPS, LOCAL), (3, 0, 2, 1, 4)
    ).reshape(GROUPS, 9, rows, 3 * LOCAL)
    packed = jnp.pad(packed, ((0, 0), (0, 0), (0, 0), (0, HALO - 3 * LOCAL)))
    vmem = pl.BlockSpec(memory_space=pltpu.VMEM)
    half = CH_IN // 2
    out, gin, fgrad = pl.pallas_call(
        lambda *refs: fused_kernel(1.0 / math.sqrt(cells), *refs),
        out_shape=(
            jax.ShapeDtypeStruct((depth_dev, LOCAL, PLANE), jnp.bfloat16),
            jax.ShapeDtypeStruct((depth_dev, LOCAL, PLANE), jnp.bfloat16),
            jax.ShapeDtypeStruct((27, rows, CH_IN), jnp.float32),
        ),
        in_specs=[vmem] * 4,
        out_specs=(vmem,) * 3,
        scratch_shapes=[
            pltpu.VMEM((4, 3, CH_IN, PLANE), jnp.bfloat16),
            pltpu.VMEM((4, 3, CH_OUT, PLANE), jnp.bfloat16),
            pltpu.VMEM((2, 4, CH_IN, HALO), jnp.bfloat16),
            pltpu.VMEM((2, 2, LOCAL, HALO), jnp.bfloat16),
            pltpu.VMEM((27, LOCAL, CH_IN), jnp.bfloat16),
            pltpu.VMEM((9, CH_OUT, HALO), jnp.bfloat16),
            pltpu.VMEM((2, 3 * LOCAL, PLANE), jnp.bfloat16),
            pltpu.VMEM((2, 2, 27, rows, half), jnp.float32),
            pltpu.VMEM((2, 27, rows, half), jnp.float32),
            pltpu.VMEM((27, rows, half), jnp.float32),
            pltpu.VMEM((27, rows, half), jnp.float32),
            pltpu.VMEM((27, rows, half), jnp.float32),
            pltpu.VMEM((27, rows, half), jnp.float32),
            pltpu.SemaphoreType.DMA((44,)),
            pltpu.SemaphoreType.DMA((44,)),
        ],
        compiler_params=pltpu.CompilerParams(
            collective_id=0, has_side_effects=True, vmem_limit_bytes=40 * 2**20
        ),
    )(
        jnp.transpose(activations, (1, 0, 2)),
        jnp.transpose(grad_out, (1, 0, 2)),
        weights,
        packed,
    )
    return (jnp.transpose(out, (1, 0, 2)), jnp.transpose(gin, (1, 0, 2)), fgrad)


def solution(mesh):
    paired = mesh.shape["filt"] == 2 * GROUPS and mesh.shape["slab"] == 2
    body = per_device_paired if paired else per_device_general
    in_specs = (P("filt", "slab", None), P("filt", "slab", None), P(None, "filt", None))
    out_specs = (P("filt", "slab", None), P("filt", "slab", None), P(None, "filt", None))
    return jax.shard_map(
        body, mesh=mesh, in_specs=in_specs, out_specs=out_specs, check_vma=False
    )
```

```python
import math

import jax
import jax.numpy as jnp
from jax import lax
from jax.experimental import pallas as pl
from jax.experimental.pallas import tpu as pltpu
from jax.sharding import PartitionSpec as P

CH_IN = 256
CH_OUT = 256
GROUPS = 8
ROWS = 8
WIDTH = 64


def extended(shard, sides, width):
    for axis, dim in sides:
        count, length = (lax.axis_size(axis), shard.shape[dim])
        up = [(i, (i + 1) % count) for i in range(count - 1)]
        down = [(j, i) for i, j in up]
        last = lax.slice_in_dim(shard, length - width, length, axis=dim)
        initial = lax.slice_in_dim(shard, 0, width, axis=dim)
        before = lax.ppermute(last, axis, up)
        after = lax.ppermute(initial, axis, down)
        shard = jnp.concatenate([before, shard, after], axis=dim)
    return shard


def shifted(block, axis, distance):
    devices = range(lax.axis_size(axis))
    route = [(i - distance, i) for i in devices if i - distance in devices]
    return lax.ppermute(block, axis, route)


def from_partner(value, axis, apart):
    mask = 2**apart
    pairs = [(source, source ^ mask) for source in range(lax.axis_size(axis))]
    return lax.ppermute(value, axis, pairs)


def correlate(image, kernel, lhs_spec):
    return lax.conv_general_dilated(
        image,
        kernel,
        (1, 1, 1),
        ((0, 0), (0, 0), (1, 1)),
        dimension_numbers=(lhs_spec, "OIDHW", "NCDHW"),
        preferred_element_type=jnp.float32,
    )


def pad_block(pieces):
    chan_count = pieces.shape[0]
    depth_dev = pieces.shape[1]
    deepened = extended(pieces, (("slab", 1),), 1)
    planes_grid = deepened.reshape(chan_count, depth_dev + 2, ROWS, WIDTH)
    blocks_all = lax.axis_size("filt") // GROUPS
    row_pos = lax.axis_index("filt") // GROUPS
    from_below = shifted(planes_grid[:, :, ROWS - 1 :], "filt", GROUPS)
    from_above = shifted(planes_grid[:, :, :1], "filt", -GROUPS)
    from_below = jnp.where(row_pos == 0, jnp.zeros_like(from_below), from_below)
    from_above = jnp.where(row_pos == blocks_all - 1, jnp.zeros_like(from_above), from_above)
    return jnp.concatenate([from_below, planes_grid, from_above], axis=2)


def gather_groups(pieces):
    my_index = lax.axis_index("filt")
    for bit_num in range(GROUPS.bit_length() - 1):
        partner = from_partner(pieces, "filt", bit_num)
        upper_side = my_index // (1 << bit_num) % 2 == 1
        lower_part = jnp.where(upper_side, partner, pieces)
        upper_part = jnp.where(upper_side, pieces, partner)
        pieces = jnp.concatenate([lower_part, upper_part], axis=0)
    return pieces


def gather_blocks(pieces, axis_dim):
    blocks_all = lax.axis_size("filt") // GROUPS
    group_bits = GROUPS.bit_length() - 1
    my_index = lax.axis_index("filt")
    for section_num in range(blocks_all.bit_length() - 1):
        bit_num = group_bits + section_num
        partner = from_partner(pieces, "filt", bit_num)
        upper_side = my_index // (1 << bit_num) % 2 == 1
        lower_part = jnp.where(upper_side, partner, pieces)
        upper_part = jnp.where(upper_side, pieces, partner)
        pieces = jnp.concatenate([lower_part, upper_part], axis=axis_dim)
    return pieces


def reduce_halves(partial_value):
    blocks_all = lax.axis_size("filt") // GROUPS
    bits_count = blocks_all.bit_length() - 1
    group_bits = GROUPS.bit_length() - 1
    my_index = lax.axis_index("filt")
    for section_num in range(bits_count):
        bit_num = group_bits + bits_count - 1 - section_num
        half_size = partial_value.shape[1] // 2
        lower_part = partial_value[:, :half_size]
        upper_part = partial_value[:, half_size:]
        upper_side = my_index // (1 << bit_num) % 2 == 1
        sending = jnp.where(upper_side, lower_part, upper_part)
        keeping = jnp.where(upper_side, upper_part, lower_part)
        partial_value = keeping + from_partner(sending, "filt", bit_num)
    return partial_value


def per_device_general(activations, grad_out, weights):
    chan_local = activations.shape[0]
    depth_dev = activations.shape[1]
    blocks_all = lax.axis_size("filt") // GROUPS
    rows_dev = weights.shape[1]
    depth_all = depth_dev * lax.axis_size("slab")
    height_all = ROWS * blocks_all
    whole_in = gather_groups(pad_block(activations))
    whole_grad = gather_groups(pad_block(grad_out))
    group_weights = gather_blocks(weights, 1)
    reordered = jnp.transpose(
        weights.reshape(27, rows_dev, GROUPS, blocks_all, rows_dev), (0, 1, 3, 2, 4)
    ).reshape(27, rows_dev, CH_IN)
    stored_rows = gather_blocks(
        lax.all_to_all(reordered, "filt", split_axis=2, concat_axis=1, tiled=True), 2
    )
    column_weights = jnp.transpose(
        stored_rows.reshape(27, blocks_all, GROUPS, rows_dev, chan_local), (0, 2, 1, 3, 4)
    ).reshape(27, CH_OUT, chan_local)
    out_kernel = jnp.transpose(group_weights, (1, 2, 0)).reshape(chan_local, CH_IN, 3, 3, 3)
    output_sum = correlate(whole_in[None], out_kernel, "NCDHW")
    grad_kernel = grad_out.reshape(chan_local, 1, depth_dev, ROWS, WIDTH)
    filter_terms = correlate(whole_in[:, None], grad_kernel, "NCDHW")
    filter_part = jnp.transpose(filter_terms.reshape(CH_IN, chan_local, 27), (2, 1, 0))
    in_kernel = jnp.transpose(column_weights[::-1], (2, 1, 0)).reshape(chan_local, CH_OUT, 3, 3, 3)
    input_sum = correlate(whole_grad[None], in_kernel, "NCDHW")
    scale_factor = 1.0 / math.sqrt(depth_all * height_all * WIDTH)
    filter_grad = lax.psum(reduce_halves(filter_part), "slab") * scale_factor
    out_map = output_sum.astype(jnp.bfloat16).reshape(chan_local, depth_dev, ROWS * WIDTH)
    grad_in = input_sum.astype(jnp.bfloat16).reshape(chan_local, depth_dev, ROWS * WIDTH)
    return (out_map, grad_in, filter_grad)


PLANE = ROWS * WIDTH
LOCAL = CH_IN // GROUPS
HALO = 128
MESH = pl.DeviceIdType.MESH


def spread(total, low_from):
    column = lax.broadcasted_iota(jnp.int32, (LOCAL, PLANE), 1) % WIDTH
    first, middle, last = (total[k * LOCAL : (k + 1) * LOCAL] for k in range(3))
    if not low_from:
        first, last = last, first
    up = jnp.where(column == 0, 0.0, pltpu.roll(first, 1, 1))
    down = jnp.where(column == WIDTH - 1, 0.0, pltpu.roll(last, PLANE - 1, 1))
    return up + middle + down


def fused_kernel(
    scale, act, grad, own_w, out, gin, fgrad,
    own_wt, vol_in, vol_grad, halo, halo_own, group_w, column_w, shifts,
    terms, terms_core, cross_out, cross_in, half_own, half_in,
    send, recv,
):
    me = lax.axis_index("filt")
    slab = lax.axis_index("slab")
    block, group = me // GROUPS, me % GROUPS
    other_slab = 1 - slab
    across = (1 - block) * GROUPS + group
    rows = own_w.shape[1]

    def remote(src, dst, sem, filt, core):
        return pltpu.make_async_remote_copy(
            src_ref=src, dst_ref=dst, send_sem=send.at[sem], recv_sem=recv.at[sem],
            device_id=(filt, core), device_id_type=MESH,
        )

    def aligned(index, size):
        return pl.ds(pl.multiple_of(index * size, size), size)

    quad, level = group % 4, group // 4
    above = block * GROUPS + (1 - level) * 4 + quad
    square = [block * GROUPS + level * 4 + (quad + k) % 4 for k in range(1, 4)]
    others = [(me + k) % (2 * GROUPS) for k in range(1, 2 * GROUPS)]
    barrier = pltpu.get_barrier_semaphore()
    for device in others:
        pl.semaphore_signal(barrier, inc=1, device_id=(device, slab), device_id_type=MESH)
    pl.semaphore_signal(barrier, inc=1, device_id=(me, other_slab), device_id_type=MESH)

    channels = aligned(group, LOCAL)
    edge = pl.ds(pl.multiple_of((1 - block) * (PLANE - HALO), HALO), HALO)
    halo_own[0] = act[:, :, edge]
    halo_own[1] = grad[:, :, edge]
    taps = own_w[...].reshape(9, 3, rows, CH_IN)
    blank = jnp.zeros((9, rows, HALO - 3 * LOCAL), jnp.bfloat16)
    for dest in range(GROUPS):
        part = slice(dest * LOCAL, (dest + 1) * LOCAL)
        own_wt[dest] = jnp.concatenate([taps[:, c, :, part] for c in range(3)] + [blank], axis=-1)
    pl.semaphore_wait(barrier, 2 * GROUPS)

    channels_above = aligned((1 - level) * 4 + quad, LOCAL)

    def spreading(src, view, first):
        lift = remote(src, view(channels), first, above, slab)
        near = [remote(src, view(channels), first + 1 + k, d, slab) for k, d in enumerate(square)]
        passed = [
            remote(view(channels_above), view(channels_above), first + 4 + k, d, slab)
            for k, d in enumerate(square)
        ]
        return lift, near, passed

    halo_copy = remote(halo_own, halo.at[:, 1:3, channels, :], 0, across, slab)
    halo_copy.start()
    act_lift, act_near, act_passed = spreading(act, lambda c: vol_in.at[1:3, 1, c, :], 8)
    grad_lift, grad_near, grad_passed = spreading(grad, lambda c: vol_grad.at[1:3, 1, c, :], 15)
    halo_lift, halo_near, halo_passed = spreading(
        halo.at[:, 1:3, channels, :], lambda c: halo.at[:, 1:3, c, :], 1
    )
    act_lift.start()
    for copy in act_near:
        copy.start()
    half = CH_IN // 2
    side_lanes = aligned(slab, half)
    group_copy = remote(
        own_w.at[:, :, side_lanes], group_w.at[:, aligned(block, rows), side_lanes], 22, across, slab
    )
    group_copy.start()
    mine = aligned(group * 2 + block, rows)
    column_copies, column_passed = [], []
    for k in range(1, GROUPS):
        dest = (me + 2 * k + slab) % (2 * GROUPS)
        column_copies.append(
            remote(own_wt.at[dest % GROUPS], column_w.at[:, mine, :], 22 + k, dest, slab)
        )
        origin = (me + 2 * GROUPS - 2 * k - slab + 2 * GROUPS) % (2 * GROUPS)
        theirs = column_w.at[:, aligned(origin % GROUPS * 2 + origin // GROUPS, rows), :]
        column_passed.append(remote(theirs, theirs, 30 + k, me, other_slab))
    column_next = remote(own_wt.at[others[0] % GROUPS], column_w.at[:, mine, :], 30, others[0], slab)
    for copy in column_copies + [column_next]:
        copy.start()

    zero_plane = 3 * slab
    vol_in[zero_plane, 1] = jnp.zeros((CH_IN, PLANE), jnp.bfloat16)
    vol_grad[zero_plane, 1] = jnp.zeros((CH_IN, PLANE), jnp.bfloat16)
    halo[:, zero_plane] = jnp.zeros((2, CH_IN, HALO), jnp.bfloat16)
    vol_in[1:3, 1, channels, :] = act[...]
    vol_grad[1:3, 1, channels, :] = grad[...]
    group_w[:, aligned(block, rows), :] = own_w[...]
    column_w[:, mine, :] = own_wt[group]
    column = lax.broadcasted_iota(jnp.int32, (LOCAL, PLANE), 1) % WIDTH
    for depth in range(2):
        value = grad[depth].astype(jnp.float32)
        lower = jnp.where(column == WIDTH - 1, 0.0, pltpu.roll(value, PLANE - 1, 1))
        upper = jnp.where(column == 0, 0.0, pltpu.roll(value, 1, 1))
        shifts[depth, 0:LOCAL] = lower.astype(jnp.bfloat16)
        shifts[depth, LOCAL : 2 * LOCAL] = grad[depth]
        shifts[depth, 2 * LOCAL :] = upper.astype(jnp.bfloat16)

    halo_copy.wait_recv()
    halo_lift.start()
    for copy in halo_near:
        copy.start()
    act_lift.wait_recv()
    for copy in act_passed:
        copy.start()
    halo_lift.wait_recv()
    for copy in halo_passed:
        copy.start()
    grad_lift.start()
    for copy in grad_near:
        copy.start()

    gives, takes = 2 - slab, 3 * slab
    for copy in act_near + act_passed:
        copy.wait_recv()
    act_plane = remote(vol_in.at[gives, 1], vol_in.at[takes, 1], 38, me, other_slab)
    act_plane.start()
    for copy in halo_near + halo_passed:
        copy.wait_recv()
    halo_plane = remote(halo.at[:, gives], halo.at[:, takes], 39, me, other_slab)
    halo_plane.start()
    grad_lift.wait_recv()
    for copy in grad_passed:
        copy.start()

    def shift_rows(volume, which, plane):
        edges = halo[which, plane]
        none = jnp.zeros_like(edges)
        whole = jnp.concatenate(
            [jnp.where(block == 1, edges, none), volume[plane, 1], jnp.where(block == 0, edges, none)],
            axis=1,
        )
        volume[plane, 0] = whole[:, HALO - WIDTH : HALO - WIDTH + PLANE]
        volume[plane, 2] = whole[:, HALO + WIDTH : HALO + WIDTH + PLANE]

    shift_rows(vol_in, 0, 1)
    shift_rows(vol_in, 0, 2)
    act_plane.wait_recv()
    halo_plane.wait_recv()
    shift_rows(vol_in, 0, 0)
    shift_rows(vol_in, 0, 3)

    over_cells = (((1,), (1,)), ((), ()))
    def part(a):
        return pl.ds(9 * a, 9)

    terms_copies = [
        remote(terms.at[other_slab, :, part(a)], terms_core.at[:, part(a)], 41 + a, me, other_slab)
        for a in range(3)
    ]
    crossing = [
        remote(cross_out.at[part(a)], cross_in.at[part(a)], 45 + a, across, slab) for a in range(3)
    ]

    def cross(a):
        terms_copies[a].wait_recv()
        cross_out[part(a)] = terms[slab, 1 - block, part(a)] + terms_core[1 - block, part(a)]
        crossing[a].start()

    for a in range(3):
        for b in range(3):
            total = sum(
                lax.dot_general(
                    shifts[depth], vol_in[depth + a, b], over_cells,
                    preferred_element_type=jnp.float32,
                )
                for depth in range(2)
            )
            for c in range(3):
                for dest in range(2):
                    low = c * LOCAL + dest * rows
                    for side in range(2):
                        terms[side, dest, 9 * a + 3 * b + c] = total[
                            low : low + rows, side * half : (side + 1) * half
                        ]
        terms_copies[a].start()
        if a > 0:
            cross(a - 1)

    group_copy.wait_recv()
    arrived = group_w.at[:, aligned(1 - block, rows), side_lanes]
    group_passed = remote(arrived, arrived, 44, me, other_slab)
    group_passed.start()
    cross(2)
    group_passed.wait_recv()
    for depth in range(2):
        total = jnp.zeros((3 * LOCAL, PLANE), jnp.float32)
        for pair in range(9):
            filters = group_w[3 * pair : 3 * pair + 3].reshape(3 * LOCAL, CH_IN)
            total += jnp.dot(
                filters, vol_in[depth + pair // 3, pair % 3], preferred_element_type=jnp.float32
            )
        out[depth] = spread(total, True).astype(out.dtype)

    for copy, onward in zip(column_copies, column_passed):
        copy.wait_recv()
        onward.start()
    for copy in grad_near + grad_passed:
        copy.wait_recv()
    grad_plane = remote(vol_grad.at[gives, 1], vol_grad.at[takes, 1], 40, me, other_slab)
    grad_plane.start()
    shift_rows(vol_grad, 1, 1)
    shift_rows(vol_grad, 1, 2)
    grad_plane.wait_recv()
    shift_rows(vol_grad, 1, 0)
    shift_rows(vol_grad, 1, 3)
    for copy in column_passed + [column_next]:
        copy.wait_recv()
    over_rows = (((0,), (0,)), ((), ()))
    totals = [jnp.zeros((HALO, PLANE), jnp.float32) for _ in range(2)]
    for pair in range(9):
        filters = column_w[pair]
        for depth in range(2):
            totals[depth] += lax.dot_general(
                filters, vol_grad[depth + 2 - pair // 3, 2 - pair % 3], over_rows,
                preferred_element_type=jnp.float32,
            )
    for depth in range(2):
        gin[depth] = spread(totals[depth], False).astype(gin.dtype)

    shares = [
        remote(half_own.at[part(a)], half_in.at[part(a)], 48 + a, me, other_slab) for a in range(3)
    ]
    for a in range(3):
        crossing[a].wait_recv()
        mean = (terms[slab, block, part(a)] + terms_core[block, part(a)] + cross_in[part(a)]) * scale
        half_own[part(a)] = mean
        shares[a].start()
        fgrad[part(a), :, side_lanes] = mean
    for copy in shares:
        copy.wait_recv()
    fgrad[:, :, aligned(other_slab, half)] = half_in[...]

    for copy in (
        [halo_copy, group_copy, group_passed, act_plane, halo_plane, grad_plane, column_next]
        + [act_lift, grad_lift, halo_lift]
        + act_near + act_passed + grad_near + grad_passed + halo_near + halo_passed
        + column_copies + column_passed + terms_copies + crossing + shares
    ):
        copy.wait_send()


def per_device_paired(activations, grad_out, weights):
    depth_dev = activations.shape[1]
    rows = weights.shape[1]
    cells = depth_dev * 2 * ROWS * 2 * WIDTH
    vmem = pl.BlockSpec(memory_space=pltpu.VMEM)
    half = CH_IN // 2
    out, gin, fgrad = pl.pallas_call(
        lambda *refs: fused_kernel(1.0 / math.sqrt(cells), *refs),
        out_shape=(
            jax.ShapeDtypeStruct((depth_dev, LOCAL, PLANE), jnp.bfloat16),
            jax.ShapeDtypeStruct((depth_dev, LOCAL, PLANE), jnp.bfloat16),
            jax.ShapeDtypeStruct((27, rows, CH_IN), jnp.float32),
        ),
        in_specs=[vmem] * 3,
        out_specs=(vmem,) * 3,
        scratch_shapes=[
            pltpu.VMEM((GROUPS, 9, rows, HALO), jnp.bfloat16),
            pltpu.VMEM((4, 3, CH_IN, PLANE), jnp.bfloat16),
            pltpu.VMEM((4, 3, CH_OUT, PLANE), jnp.bfloat16),
            pltpu.VMEM((2, 4, CH_IN, HALO), jnp.bfloat16),
            pltpu.VMEM((2, 2, LOCAL, HALO), jnp.bfloat16),
            pltpu.VMEM((27, LOCAL, CH_IN), jnp.bfloat16),
            pltpu.VMEM((9, CH_OUT, HALO), jnp.bfloat16),
            pltpu.VMEM((2, 3 * LOCAL, PLANE), jnp.bfloat16),
            pltpu.VMEM((2, 2, 27, rows, half), jnp.float32),
            pltpu.VMEM((2, 27, rows, half), jnp.float32),
            pltpu.VMEM((27, rows, half), jnp.float32),
            pltpu.VMEM((27, rows, half), jnp.float32),
            pltpu.VMEM((27, rows, half), jnp.float32),
            pltpu.VMEM((27, rows, half), jnp.float32),
            pltpu.SemaphoreType.DMA((51,)),
            pltpu.SemaphoreType.DMA((51,)),
        ],
        compiler_params=pltpu.CompilerParams(
            collective_id=0, has_side_effects=True, vmem_limit_bytes=40 * 2**20
        ),
    )(
        jnp.transpose(activations, (1, 0, 2)),
        jnp.transpose(grad_out, (1, 0, 2)),
        weights,
    )
    return (jnp.transpose(out, (1, 0, 2)), jnp.transpose(gin, (1, 0, 2)), fgrad)


def solution(mesh):
    paired = mesh.shape["filt"] == 2 * GROUPS and mesh.shape["slab"] == 2
    body = per_device_paired if paired else per_device_general
    in_specs = (P("filt", "slab", None), P("filt", "slab", None), P(None, "filt", None))
    out_specs = (P("filt", "slab", None), P("filt", "slab", None), P(None, "filt", None))
    return jax.shard_map(
        body, mesh=mesh, in_specs=in_specs, out_specs=out_specs, check_vma=False
    )
```

```python
import math

import jax
import jax.numpy as jnp
from jax import lax
from jax.experimental import pallas as pl
from jax.experimental.pallas import tpu as pltpu
from jax.sharding import PartitionSpec as P

CH_IN = 256
CH_OUT = 256
GROUPS = 8
ROWS = 8
WIDTH = 64


def extended(shard, sides, width):
    for axis, dim in sides:
        count, length = (lax.axis_size(axis), shard.shape[dim])
        up = [(i, (i + 1) % count) for i in range(count - 1)]
        down = [(j, i) for i, j in up]
        last = lax.slice_in_dim(shard, length - width, length, axis=dim)
        initial = lax.slice_in_dim(shard, 0, width, axis=dim)
        before = lax.ppermute(last, axis, up)
        after = lax.ppermute(initial, axis, down)
        shard = jnp.concatenate([before, shard, after], axis=dim)
    return shard


def shifted(block, axis, distance):
    devices = range(lax.axis_size(axis))
    route = [(i - distance, i) for i in devices if i - distance in devices]
    return lax.ppermute(block, axis, route)


def from_partner(value, axis, apart):
    mask = 2**apart
    pairs = [(source, source ^ mask) for source in range(lax.axis_size(axis))]
    return lax.ppermute(value, axis, pairs)


def correlate(image, kernel, lhs_spec):
    return lax.conv_general_dilated(
        image,
        kernel,
        (1, 1, 1),
        ((0, 0), (0, 0), (1, 1)),
        dimension_numbers=(lhs_spec, "OIDHW", "NCDHW"),
        preferred_element_type=jnp.float32,
    )


def pad_block(pieces):
    chan_count = pieces.shape[0]
    depth_dev = pieces.shape[1]
    deepened = extended(pieces, (("slab", 1),), 1)
    planes_grid = deepened.reshape(chan_count, depth_dev + 2, ROWS, WIDTH)
    blocks_all = lax.axis_size("filt") // GROUPS
    row_pos = lax.axis_index("filt") // GROUPS
    from_below = shifted(planes_grid[:, :, ROWS - 1 :], "filt", GROUPS)
    from_above = shifted(planes_grid[:, :, :1], "filt", -GROUPS)
    from_below = jnp.where(row_pos == 0, jnp.zeros_like(from_below), from_below)
    from_above = jnp.where(row_pos == blocks_all - 1, jnp.zeros_like(from_above), from_above)
    return jnp.concatenate([from_below, planes_grid, from_above], axis=2)


def gather_groups(pieces):
    my_index = lax.axis_index("filt")
    for bit_num in range(GROUPS.bit_length() - 1):
        partner = from_partner(pieces, "filt", bit_num)
        upper_side = my_index // (1 << bit_num) % 2 == 1
        lower_part = jnp.where(upper_side, partner, pieces)
        upper_part = jnp.where(upper_side, pieces, partner)
        pieces = jnp.concatenate([lower_part, upper_part], axis=0)
    return pieces


def gather_blocks(pieces, axis_dim):
    blocks_all = lax.axis_size("filt") // GROUPS
    group_bits = GROUPS.bit_length() - 1
    my_index = lax.axis_index("filt")
    for section_num in range(blocks_all.bit_length() - 1):
        bit_num = group_bits + section_num
        partner = from_partner(pieces, "filt", bit_num)
        upper_side = my_index // (1 << bit_num) % 2 == 1
        lower_part = jnp.where(upper_side, partner, pieces)
        upper_part = jnp.where(upper_side, pieces, partner)
        pieces = jnp.concatenate([lower_part, upper_part], axis=axis_dim)
    return pieces


def reduce_halves(partial_value):
    blocks_all = lax.axis_size("filt") // GROUPS
    bits_count = blocks_all.bit_length() - 1
    group_bits = GROUPS.bit_length() - 1
    my_index = lax.axis_index("filt")
    for section_num in range(bits_count):
        bit_num = group_bits + bits_count - 1 - section_num
        half_size = partial_value.shape[1] // 2
        lower_part = partial_value[:, :half_size]
        upper_part = partial_value[:, half_size:]
        upper_side = my_index // (1 << bit_num) % 2 == 1
        sending = jnp.where(upper_side, lower_part, upper_part)
        keeping = jnp.where(upper_side, upper_part, lower_part)
        partial_value = keeping + from_partner(sending, "filt", bit_num)
    return partial_value


def per_device_general(activations, grad_out, weights):
    chan_local = activations.shape[0]
    depth_dev = activations.shape[1]
    blocks_all = lax.axis_size("filt") // GROUPS
    rows_dev = weights.shape[1]
    depth_all = depth_dev * lax.axis_size("slab")
    height_all = ROWS * blocks_all
    whole_in = gather_groups(pad_block(activations))
    whole_grad = gather_groups(pad_block(grad_out))
    group_weights = gather_blocks(weights, 1)
    reordered = jnp.transpose(
        weights.reshape(27, rows_dev, GROUPS, blocks_all, rows_dev), (0, 1, 3, 2, 4)
    ).reshape(27, rows_dev, CH_IN)
    stored_rows = gather_blocks(
        lax.all_to_all(reordered, "filt", split_axis=2, concat_axis=1, tiled=True), 2
    )
    column_weights = jnp.transpose(
        stored_rows.reshape(27, blocks_all, GROUPS, rows_dev, chan_local), (0, 2, 1, 3, 4)
    ).reshape(27, CH_OUT, chan_local)
    out_kernel = jnp.transpose(group_weights, (1, 2, 0)).reshape(chan_local, CH_IN, 3, 3, 3)
    output_sum = correlate(whole_in[None], out_kernel, "NCDHW")
    grad_kernel = grad_out.reshape(chan_local, 1, depth_dev, ROWS, WIDTH)
    filter_terms = correlate(whole_in[:, None], grad_kernel, "NCDHW")
    filter_part = jnp.transpose(filter_terms.reshape(CH_IN, chan_local, 27), (2, 1, 0))
    in_kernel = jnp.transpose(column_weights[::-1], (2, 1, 0)).reshape(chan_local, CH_OUT, 3, 3, 3)
    input_sum = correlate(whole_grad[None], in_kernel, "NCDHW")
    scale_factor = 1.0 / math.sqrt(depth_all * height_all * WIDTH)
    filter_grad = lax.psum(reduce_halves(filter_part), "slab") * scale_factor
    out_map = output_sum.astype(jnp.bfloat16).reshape(chan_local, depth_dev, ROWS * WIDTH)
    grad_in = input_sum.astype(jnp.bfloat16).reshape(chan_local, depth_dev, ROWS * WIDTH)
    return (out_map, grad_in, filter_grad)


PLANE = ROWS * WIDTH
LOCAL = CH_IN // GROUPS
HALO = 128
MESH = pl.DeviceIdType.MESH


def spread(total, low_from):
    column = lax.broadcasted_iota(jnp.int32, (LOCAL, PLANE), 1) % WIDTH
    first, middle, last = (total[k * LOCAL : (k + 1) * LOCAL] for k in range(3))
    if not low_from:
        first, last = last, first
    up = jnp.where(column == 0, 0.0, pltpu.roll(first, 1, 1))
    down = jnp.where(column == WIDTH - 1, 0.0, pltpu.roll(last, PLANE - 1, 1))
    return up + middle + down


def fused_kernel(
    scale, act, grad, own_w, out, gin, fgrad,
    own_wt, vol_in, vol_grad, halo, halo_own, group_w, column_w, shifts,
    terms, terms_core, cross_out, cross_in, half_own, half_in,
    send, recv,
):
    me = lax.axis_index("filt")
    slab = lax.axis_index("slab")
    block, group = me // GROUPS, me % GROUPS
    other_slab = 1 - slab
    across = (1 - block) * GROUPS + group
    rows = own_w.shape[1]

    def remote(src, dst, sem, filt, core):
        return pltpu.make_async_remote_copy(
            src_ref=src, dst_ref=dst, send_sem=send.at[sem], recv_sem=recv.at[sem],
            device_id=(filt, core), device_id_type=MESH,
        )

    def aligned(index, size):
        return pl.ds(pl.multiple_of(index * size, size), size)

    quad, level = group % 4, group // 4
    above = block * GROUPS + (1 - level) * 4 + quad
    square = [block * GROUPS + level * 4 + (quad + k) % 4 for k in range(1, 4)]
    others = [(me + k) % (2 * GROUPS) for k in range(1, 2 * GROUPS)]
    barrier = pltpu.get_barrier_semaphore()
    for device in others:
        pl.semaphore_signal(barrier, inc=1, device_id=(device, slab), device_id_type=MESH)
    pl.semaphore_signal(barrier, inc=1, device_id=(me, other_slab), device_id_type=MESH)

    channels = aligned(group, LOCAL)
    edge = pl.ds(pl.multiple_of((1 - block) * (PLANE - HALO), HALO), HALO)
    halo_own[0] = act[:, :, edge]
    halo_own[1] = grad[:, :, edge]
    taps = own_w[...].reshape(9, 3, rows, CH_IN)
    blank = jnp.zeros((9, rows, HALO - 3 * LOCAL), jnp.bfloat16)
    for dest in range(GROUPS):
        part = slice(dest * LOCAL, (dest + 1) * LOCAL)
        own_wt[dest] = jnp.concatenate([taps[:, c, :, part] for c in range(3)] + [blank], axis=-1)
    pl.semaphore_wait(barrier, 2 * GROUPS)

    channels_above = aligned((1 - level) * 4 + quad, LOCAL)

    def spreading(src, view, first):
        lift = remote(src, view(channels), first, above, slab)
        near = [remote(src, view(channels), first + 1 + k, d, slab) for k, d in enumerate(square)]
        passed = [
            remote(view(channels_above), view(channels_above), first + 4 + k, d, slab)
            for k, d in enumerate(square)
        ]
        return lift, near, passed

    halo_copy = remote(halo_own, halo.at[:, 1:3, channels, :], 0, across, slab)
    halo_copy.start()
    act_lift, act_near, act_passed = spreading(act, lambda c: vol_in.at[1:3, 1, c, :], 8)
    grad_lift, grad_near, grad_passed = spreading(grad, lambda c: vol_grad.at[1:3, 1, c, :], 15)
    halo_lift, halo_near, halo_passed = spreading(
        halo.at[:, 1:3, channels, :], lambda c: halo.at[:, 1:3, c, :], 1
    )
    act_lift.start()
    for copy in act_near:
        copy.start()
    grad_lift.start()
    half = CH_IN // 2
    side_lanes = aligned(slab, half)
    group_copy = remote(
        own_w.at[:, :, side_lanes], group_w.at[:, aligned(block, rows), side_lanes], 22, across, slab
    )
    group_copy.start()
    mine = aligned(group * 2 + block, rows)
    column_copies, column_passed = [], []
    for k in range(1, GROUPS):
        dest = (me + 2 * k + slab) % (2 * GROUPS)
        column_copies.append(
            remote(own_wt.at[dest % GROUPS], column_w.at[:, mine, :], 22 + k, dest, slab)
        )
        origin = (me + 2 * GROUPS - 2 * k - slab + 2 * GROUPS) % (2 * GROUPS)
        theirs = column_w.at[:, aligned(origin % GROUPS * 2 + origin // GROUPS, rows), :]
        column_passed.append(remote(theirs, theirs, 30 + k, me, other_slab))
    column_next = remote(own_wt.at[others[0] % GROUPS], column_w.at[:, mine, :], 30, others[0], slab)

    zero_plane = 3 * slab
    vol_in[zero_plane, 1] = jnp.zeros((CH_IN, PLANE), jnp.bfloat16)
    vol_grad[zero_plane, 1] = jnp.zeros((CH_IN, PLANE), jnp.bfloat16)
    halo[:, zero_plane] = jnp.zeros((2, CH_IN, HALO), jnp.bfloat16)
    vol_in[1:3, 1, channels, :] = act[...]
    vol_grad[1:3, 1, channels, :] = grad[...]
    group_w[:, aligned(block, rows), :] = own_w[...]
    column_w[:, mine, :] = own_wt[group]
    column = lax.broadcasted_iota(jnp.int32, (LOCAL, PLANE), 1) % WIDTH
    for depth in range(2):
        value = grad[depth].astype(jnp.float32)
        lower = jnp.where(column == WIDTH - 1, 0.0, pltpu.roll(value, PLANE - 1, 1))
        upper = jnp.where(column == 0, 0.0, pltpu.roll(value, 1, 1))
        shifts[depth, 0:LOCAL] = lower.astype(jnp.bfloat16)
        shifts[depth, LOCAL : 2 * LOCAL] = grad[depth]
        shifts[depth, 2 * LOCAL :] = upper.astype(jnp.bfloat16)

    halo_copy.wait_recv()
    halo_lift.start()
    for copy in halo_near:
        copy.start()
    act_lift.wait_recv()
    for copy in act_passed:
        copy.start()
    halo_lift.wait_recv()
    for copy in halo_passed:
        copy.start()
    for copy in grad_near:
        copy.start()
    for copy in column_copies + [column_next]:
        copy.start()

    gives, takes = 2 - slab, 3 * slab
    for copy in act_near + act_passed:
        copy.wait_recv()
    act_plane = remote(vol_in.at[gives, 1], vol_in.at[takes, 1], 38, me, other_slab)
    act_plane.start()
    for copy in halo_near + halo_passed:
        copy.wait_recv()
    halo_plane = remote(halo.at[:, gives], halo.at[:, takes], 39, me, other_slab)
    halo_plane.start()
    grad_lift.wait_recv()
    for copy in grad_passed:
        copy.start()

    def shift_rows(volume, which, plane):
        edges = halo[which, plane]
        none = jnp.zeros_like(edges)
        whole = jnp.concatenate(
            [jnp.where(block == 1, edges, none), volume[plane, 1], jnp.where(block == 0, edges, none)],
            axis=1,
        )
        volume[plane, 0] = whole[:, HALO - WIDTH : HALO - WIDTH + PLANE]
        volume[plane, 2] = whole[:, HALO + WIDTH : HALO + WIDTH + PLANE]

    shift_rows(vol_in, 0, 1)
    shift_rows(vol_in, 0, 2)
    act_plane.wait_recv()
    halo_plane.wait_recv()
    shift_rows(vol_in, 0, 0)
    shift_rows(vol_in, 0, 3)

    over_cells = (((1,), (1,)), ((), ()))
    def part(a):
        return pl.ds(9 * a, 9)

    terms_copies = [
        remote(terms.at[other_slab, :, part(a)], terms_core.at[:, part(a)], 41 + a, me, other_slab)
        for a in range(3)
    ]
    crossing = [
        remote(cross_out.at[part(a)], cross_in.at[part(a)], 45 + a, across, slab) for a in range(3)
    ]

    def cross(a):
        terms_copies[a].wait_recv()
        cross_out[part(a)] = terms[slab, 1 - block, part(a)] + terms_core[1 - block, part(a)]
        crossing[a].start()

    for a in range(3):
        for b in range(3):
            total = sum(
                lax.dot_general(
                    shifts[depth], vol_in[depth + a, b], over_cells,
                    preferred_element_type=jnp.float32,
                )
                for depth in range(2)
            )
            for c in range(3):
                for dest in range(2):
                    low = c * LOCAL + dest * rows
                    for side in range(2):
                        terms[side, dest, 9 * a + 3 * b + c] = total[
                            low : low + rows, side * half : (side + 1) * half
                        ]
        terms_copies[a].start()
        if a > 0:
            cross(a - 1)

    group_copy.wait_recv()
    arrived = group_w.at[:, aligned(1 - block, rows), side_lanes]
    group_passed = remote(arrived, arrived, 44, me, other_slab)
    group_passed.start()
    cross(2)
    group_passed.wait_recv()
    for depth in range(2):
        total = jnp.zeros((3 * LOCAL, PLANE), jnp.float32)
        for pair in range(9):
            filters = group_w[3 * pair : 3 * pair + 3].reshape(3 * LOCAL, CH_IN)
            total += jnp.dot(
                filters, vol_in[depth + pair // 3, pair % 3], preferred_element_type=jnp.float32
            )
        out[depth] = spread(total, True).astype(out.dtype)

    for copy, onward in zip(column_copies, column_passed):
        copy.wait_recv()
        onward.start()
    for copy in grad_near + grad_passed:
        copy.wait_recv()
    grad_plane = remote(vol_grad.at[gives, 1], vol_grad.at[takes, 1], 40, me, other_slab)
    grad_plane.start()
    shift_rows(vol_grad, 1, 1)
    shift_rows(vol_grad, 1, 2)
    grad_plane.wait_recv()
    shift_rows(vol_grad, 1, 0)
    shift_rows(vol_grad, 1, 3)
    for copy in column_passed + [column_next]:
        copy.wait_recv()
    over_rows = (((0,), (0,)), ((), ()))
    totals = [jnp.zeros((HALO, PLANE), jnp.float32) for _ in range(2)]
    for pair in range(9):
        filters = column_w[pair]
        for depth in range(2):
            totals[depth] += lax.dot_general(
                filters, vol_grad[depth + 2 - pair // 3, 2 - pair % 3], over_rows,
                preferred_element_type=jnp.float32,
            )
    for depth in range(2):
        gin[depth] = spread(totals[depth], False).astype(gin.dtype)

    shares = [
        remote(half_own.at[part(a)], half_in.at[part(a)], 48 + a, me, other_slab) for a in range(3)
    ]
    for a in range(3):
        crossing[a].wait_recv()
        mean = (terms[slab, block, part(a)] + terms_core[block, part(a)] + cross_in[part(a)]) * scale
        half_own[part(a)] = mean
        shares[a].start()
        fgrad[part(a), :, side_lanes] = mean
    for copy in shares:
        copy.wait_recv()
    fgrad[:, :, aligned(other_slab, half)] = half_in[...]

    for copy in (
        [halo_copy, group_copy, group_passed, act_plane, halo_plane, grad_plane, column_next]
        + [act_lift, grad_lift, halo_lift]
        + act_near + act_passed + grad_near + grad_passed + halo_near + halo_passed
        + column_copies + column_passed + terms_copies + crossing + shares
    ):
        copy.wait_send()


def per_device_paired(activations, grad_out, weights):
    depth_dev = activations.shape[1]
    rows = weights.shape[1]
    cells = depth_dev * 2 * ROWS * 2 * WIDTH
    vmem = pl.BlockSpec(memory_space=pltpu.VMEM)
    half = CH_IN // 2
    out, gin, fgrad = pl.pallas_call(
        lambda *refs: fused_kernel(1.0 / math.sqrt(cells), *refs),
        out_shape=(
            jax.ShapeDtypeStruct((depth_dev, LOCAL, PLANE), jnp.bfloat16),
            jax.ShapeDtypeStruct((depth_dev, LOCAL, PLANE), jnp.bfloat16),
            jax.ShapeDtypeStruct((27, rows, CH_IN), jnp.float32),
        ),
        in_specs=[vmem] * 3,
        out_specs=(vmem,) * 3,
        scratch_shapes=[
            pltpu.VMEM((GROUPS, 9, rows, HALO), jnp.bfloat16),
            pltpu.VMEM((4, 3, CH_IN, PLANE), jnp.bfloat16),
            pltpu.VMEM((4, 3, CH_OUT, PLANE), jnp.bfloat16),
            pltpu.VMEM((2, 4, CH_IN, HALO), jnp.bfloat16),
            pltpu.VMEM((2, 2, LOCAL, HALO), jnp.bfloat16),
            pltpu.VMEM((27, LOCAL, CH_IN), jnp.bfloat16),
            pltpu.VMEM((9, CH_OUT, HALO), jnp.bfloat16),
            pltpu.VMEM((2, 3 * LOCAL, PLANE), jnp.bfloat16),
            pltpu.VMEM((2, 2, 27, rows, half), jnp.float32),
            pltpu.VMEM((2, 27, rows, half), jnp.float32),
            pltpu.VMEM((27, rows, half), jnp.float32),
            pltpu.VMEM((27, rows, half), jnp.float32),
            pltpu.VMEM((27, rows, half), jnp.float32),
            pltpu.VMEM((27, rows, half), jnp.float32),
            pltpu.SemaphoreType.DMA((51,)),
            pltpu.SemaphoreType.DMA((51,)),
        ],
        compiler_params=pltpu.CompilerParams(
            collective_id=0, has_side_effects=True, vmem_limit_bytes=40 * 2**20
        ),
    )(
        jnp.transpose(activations, (1, 0, 2)),
        jnp.transpose(grad_out, (1, 0, 2)),
        weights,
    )
    return (jnp.transpose(out, (1, 0, 2)), jnp.transpose(gin, (1, 0, 2)), fgrad)


def solution(mesh):
    paired = mesh.shape["filt"] == 2 * GROUPS and mesh.shape["slab"] == 2
    body = per_device_paired if paired else per_device_general
    in_specs = (P("filt", "slab", None), P("filt", "slab", None), P(None, "filt", None))
    out_specs = (P("filt", "slab", None), P("filt", "slab", None), P(None, "filt", None))
    return jax.shard_map(
        body, mesh=mesh, in_specs=in_specs, out_specs=out_specs, check_vma=False
    )
```
